512 devices in a mesh: dp: 32 (over x, z_lo, core), seq: 16 (over z_hi, y).
Axes of the slice: x: 4, y: 4, z: 16 (z_hi: 4, z_lo: 4; z = z_hi * 4 + z_lo), core: 2. Of those that a mesh axis runs over, the one named last changes fastest.
Arguments:
- activations: bfloat16 [32, 2048, 1536], P('dp', 'seq'), may hold values from -6 to 6
- norm_gain: float32 [1536], replicated, may hold values from 0.25 to 1.75
- w_query: bfloat16 [1536, 1024], P('dp'), as said below
- w_key: bfloat16 [1536, 128], P('dp'), as said below
- w_value: bfloat16 [1536, 192], P('dp'), may hold values from -0.15625 to 0.15625
- w_out: bfloat16 [1536, 1536], P('dp'), may hold values from -0.15625 to 0.15625
- cotangent: bfloat16 [32, 2048, 1536], P('dp', 'seq'), may hold values from -6 to 6
Outputs:
- layer_out: bfloat16 [32, 2048, 1536], P('dp', 'seq')
- input_grad: bfloat16 [32, 2048, 1536], P('dp', 'seq')
- key_value_grad: float32 [1536, 320], P('dp')
The draws below stay inside these ranges and needn't reach their ends.
Inputs may be any that keep to these rules, and one draw needn't show every extreme that they name: `w_query`: a projection matrix of full rank. `w_key`: a projection matrix of full rank.
All inputs are finite; a program needn't handle non-finite values.
Results may differ from the reference program's by a relative error of at most 0.034.
Values may be sent and summed in bfloat16 or wider, within the bound.
A program may use at most 64 MiB of HBM per device.

```python
import jax
import jax.numpy as jnp
from jax import lax

D = 1536
HEADS = 8
HQ = 128
DV = 192
TOK_DEV = 128
LEN = 2048
WINDOWS = 32
N_SEQ = 16


def key_base(key):
    return jnp.clip(jax.random.normal(key, (D, HQ), jnp.float32), -4.0, 4.0) * D ** (-0.5)


def draw_w_key(key, part):
    base = key_base(key)
    return base.astype(jnp.bfloat16)


def draw_w_query(key, part):
    key = jax.random.fold_in(key, 5)
    noise = jnp.clip(jax.random.normal(key, (D, HEADS * HQ), jnp.float32), -4.0, 4.0) * D ** (-0.5)
    result = noise
    return result.astype(jnp.bfloat16)


def raised(array, stream_key, source, target, shards_of, factor):
    def block_of(position):
        return (jnp.arange(array.shape[position]) // (array.shape[position] // shards_of)).reshape((-1,) + (1,) * (array.ndim - 1 - position))

    first = jax.random.permutation(stream_key, shards_of)[block_of(target)]
    second = (block_of(target) + shards_of // 2) % shards_of
    return jnp.where((block_of(source) == first) | (block_of(source) == second), factor * array, array)


def steps_of(key, dims, pieces, least, high):
    def one(axis_at, shards_of):
        heights = jax.random.uniform(jax.random.fold_in(jax.random.fold_in(key, 6), axis_at), (shards_of,), jnp.float32, least / len(pieces), high / len(pieces))
        return jnp.repeat(jnp.exp(heights), dims[axis_at] // shards_of).reshape((-1,) + (1,) * (len(dims) - axis_at - 1))

    factor_of = one(*pieces[0])
    for cut in pieces[1:]:
        factor_of = factor_of * one(*cut)
    return factor_of


def scatter_about(rng, extent, spread, most, split=(), held_as=jnp.bfloat16):
    array = spread * jax.random.normal(rng, extent, jnp.float32)
    if split:
        array = array * steps_of(rng, extent, split, -0.22, 0.18)
    return jnp.clip(array, -most, most).astype(held_as)


def noise_with(stream_key, shape, scale, most, pieces, heavy, dtype=jnp.bfloat16):
    values = scale * jax.random.normal(stream_key, shape, jnp.float32)
    if pieces:
        values = values * steps_of(stream_key, shape, pieces, -0.22, 0.18)
    return jnp.clip(raised(values, jax.random.fold_in(stream_key, 3), *heavy), -most, most).astype(dtype)


def setup_inputs(seed: int = 0) -> dict:
    seeds = jax.random.split(jax.random.key(seed), 8)
    activations = noise_with(seeds[0], (WINDOWS, LEN, D), 1.0, 6.0, ((0, 32), (1, 16)), (0, 2, 32, 2.75))
    norm_gain = jnp.clip(1.0 + 0.15 * jax.random.normal(seeds[1], (D,), jnp.float32), 0.25, 1.75)
    w_query = draw_w_query(jax.random.fold_in(seeds[7], 71), 0)
    w_key = draw_w_key(jax.random.fold_in(seeds[7], 71), 0)
    w_value = scatter_about(seeds[4], (D, DV), D ** -0.5, 0.15625, ((0, 32),))
    w_out = scatter_about(seeds[5], (HEADS * DV, D), (HEADS * DV) ** -0.5, 0.15625, ((0, 32),))
    cotangent = scatter_about(seeds[6], (WINDOWS, LEN, D), 1.0, 6.0, ((0, 32), (1, 16)))
    return {"activations": activations, "norm_gain": norm_gain, "w_query": w_query, "w_key": w_key, "w_value": w_value, "w_out": w_out, "cotangent": cotangent}


epsilon = 1e-06

def window_pass(acts_win, grad_win, norm_gain, w_query, w_key, w_value, w_out):
    acts_wide = acts_win.astype(jnp.float32)
    rscale = lax.rsqrt(lax.optimization_barrier(jnp.mean(acts_wide * acts_wide, axis=-1, keepdims=True)) + epsilon)
    normed = (acts_wide * rscale * norm_gain).astype(jnp.bfloat16)
    qscale = HQ ** (-0.5)
    queries = (jnp.dot(normed, w_query, preferred_element_type=jnp.float32) * qscale).astype(jnp.bfloat16)
    keys = jnp.dot(normed, w_key, preferred_element_type=jnp.float32).astype(jnp.bfloat16)
    values = jnp.dot(normed, w_value, preferred_element_type=jnp.float32).astype(jnp.bfloat16)
    out_grad = jnp.dot(grad_win, w_out.T, preferred_element_type=jnp.float32).astype(jnp.bfloat16)
    query_groups = queries.reshape(N_SEQ, TOK_DEV * HEADS, HQ)
    grad_groups = out_grad.reshape(N_SEQ, TOK_DEV * HEADS, DV)

    def group_pass(pair):
        query_rows, grad_rows = pair
        scores = jnp.dot(query_rows, keys.T, preferred_element_type=jnp.float32)
        top = lax.optimization_barrier(jnp.max(scores, axis=-1, keepdims=True))
        expo = jnp.exp(scores - top)
        probs = expo / lax.optimization_barrier(jnp.sum(expo, axis=-1, keepdims=True))
        probs_b = probs.astype(jnp.bfloat16)
        attended = jnp.dot(probs_b, values, preferred_element_type=jnp.float32).astype(jnp.bfloat16)
        dprob = jnp.dot(grad_rows, values.T, preferred_element_type=jnp.float32)
        centre = lax.optimization_barrier(jnp.sum(probs * dprob, axis=-1, keepdims=True))
        score_grad = (probs * (dprob - centre)).astype(jnp.bfloat16)
        query_grad = (jnp.dot(score_grad, keys, preferred_element_type=jnp.float32) * qscale).astype(jnp.bfloat16)
        key_part = jnp.dot(score_grad.T, query_rows, preferred_element_type=jnp.float32).astype(jnp.bfloat16)
        value_part = jnp.dot(probs_b.T, grad_rows, preferred_element_type=jnp.float32).astype(jnp.bfloat16)
        return (attended, query_grad, key_part, value_part)
    attended, query_grad, key_part, value_part = lax.map(group_pass, (query_groups, grad_groups))
    attended = attended.reshape(LEN, HEADS * DV)
    query_grad = query_grad.reshape(LEN, HEADS * HQ)
    key_grad = lax.optimization_barrier(jnp.sum(key_part.astype(jnp.float32), axis=0)).astype(jnp.bfloat16)
    value_grad = lax.optimization_barrier(jnp.sum(value_part.astype(jnp.float32), axis=0)).astype(jnp.bfloat16)
    layer_out = (acts_wide + jnp.dot(attended, w_out, preferred_element_type=jnp.float32)).astype(jnp.bfloat16)
    normed_grad = jnp.dot(query_grad, w_query.T, preferred_element_type=jnp.float32)
    normed_grad = normed_grad + jnp.dot(key_grad, w_key.T, preferred_element_type=jnp.float32)
    normed_grad = normed_grad + jnp.dot(value_grad, w_value.T, preferred_element_type=jnp.float32)
    scaled = normed_grad * norm_gain
    inner = lax.optimization_barrier(jnp.mean(scaled * acts_wide, axis=-1, keepdims=True))
    input_grad = (grad_win.astype(jnp.float32) + rscale * (scaled - acts_wide * rscale * rscale * inner)).astype(jnp.bfloat16)
    weight_grad = jnp.concatenate([jnp.dot(normed.T, key_grad, preferred_element_type=jnp.float32), jnp.dot(normed.T, value_grad, preferred_element_type=jnp.float32)], axis=1)
    return (layer_out, input_grad, weight_grad)

def reference(activations, norm_gain, w_query, w_key, w_value, w_out, cotangent):

    def step(total, pair):
        layer_out, input_grad, weight_grad = window_pass(pair[0], pair[1], norm_gain, w_query, w_key, w_value, w_out)
        return (total + weight_grad, (layer_out, input_grad))
    start = jnp.zeros((D, HQ + DV), jnp.float32)
    total, outputs = lax.scan(step, start, (activations, cotangent))
    return (outputs[0], outputs[1], total)
```

```python
import functools
import jax
import jax.numpy as jnp
from jax import lax
from jax.experimental import pallas as pl
from jax.experimental.pallas import tpu as pltpu
from jax.sharding import PartitionSpec as P

MESH = pl.DeviceIdType.MESH
BF = jnp.bfloat16
F32 = jnp.float32
HEADS, HQ, DV = 8, 128, 192
COLS = 2944
SHARD = 48


def spot():
    dp, sq = lax.axis_index("dp"), lax.axis_index("seq")
    x, zl, c = lax.div(dp, 8), lax.div(lax.rem(dp, 8), 2), lax.rem(dp, 2)
    zh, y = lax.div(sq, 4), lax.rem(sq, 4)
    return x, y, zh * 4 + zl, c


def dev(dx=0, dy=0, dz=0, dc=0):
    x, y, z, c = spot()
    x, y = lax.rem(x + dx + 4, 4), lax.rem(y + dy + 4, 4)
    z, c = lax.rem(z + dz + 16, 16), lax.rem(c + dc, 2)
    return (x * 8 + lax.rem(z, 4) * 2 + c, lax.div(z, 4) * 4 + y)


AXES = {
    "x": ((1, 0, 0), (-1, 0, 0)),
    "y": ((0, 1, 0), (0, -1, 0)),
    "z": ((0, 0, 1), (0, 0, -1)),
    "w": ((0, 0, 4), (0, 0, -4)),
}


class Gather:
    def __init__(self, buf, row_of, rows, col, cols, halves, order, send, recv, base, twin=None):
        self.buf, self.row_of, self.rows, self.col, self.cols = buf, row_of, rows, col, cols
        self.halves, self.order, self.send, self.recv, self.base = halves, order, send, recv, base
        self.twin = twin

    def block(self, ka, kb, part=None):
        r0, nr, c0, nc = part if part else (0, self.rows, 0, self.cols)
        return self.buf.at[pl.ds(pl.multiple_of(self.row_of(ka, kb) + r0, 16), nr), pl.ds(self.col + c0, nc)]

    def copy(self, ka, kb, part, to, slot):
        ref = self.block(ka, kb, part)
        return pltpu.make_async_remote_copy(
            src_ref=ref, dst_ref=ref, send_sem=self.send, recv_sem=self.recv.at[self.base + slot],
            device_id=to, device_id_type=MESH)

    def put(self, ka, kb, part, axis, way, slot):
        if part is not None and (part[1] == 0 or part[3] == 0):
            return
        self.copy(ka, kb, part, dev(*AXES[self.order[axis]][way]), slot).start()

    def got(self, ka, kb, part, slot):
        if part is not None and (part[1] == 0 or part[3] == 0):
            return
        self.copy(ka, kb, part, dev(*AXES[self.order[0]][0]), slot).wait_recv()

    def share(self, ka, kb):
        if self.twin is None:
            return
        ref = self.block(ka, kb)
        pltpu.make_async_remote_copy(
            src_ref=ref, dst_ref=ref, send_sem=self.twin[0], recv_sem=self.twin[1],
            device_id=dev(0, 0, 0, 1), device_id_type=MESH).start()

    def first(self):
        self.put(0, 0, None, 0, 0, 0)
        self.put(0, 0, None, 0, 1, 1)
        self.second(0)
        self.share(0, 0)

    def second(self, k):
        self.put(k, 0, None, 1, 0, 4 + 4 * k)
        self.put(k, 0, None, 1, 1, 5 + 4 * k)

    def a_near(self, k, way):
        self.got(k, 0, None, 0 if k == 3 else 1)
        self.put(k, 0, self.halves[way], 0, way, 2 + way)
        self.second(k)
        self.share(k, 0)

    def a_far(self):
        self.got(2, 0, self.halves[0], 2)
        self.got(2, 0, self.halves[1], 3)
        self.second(2)
        self.share(2, 0)

    def b_near(self, k, kb, way):
        self.got(k, kb, None, 4 + 4 * k + (0 if kb == 3 else 1))
        self.put(k, kb, self.halves[way], 1, way, 6 + 4 * k + way)
        self.share(k, kb)

    def b_far(self, k):
        self.got(k, 2, self.halves[0], 6 + 4 * k)
        self.got(k, 2, self.halves[1], 7 + 4 * k)
        self.share(k, 2)

    def steps(self):
        near = lambda k: [lambda: self.b_near(k, 3, 0), lambda: self.b_near(k, 1, 1)]
        return ([self.first, lambda: self.a_near(3, 0), lambda: self.a_near(1, 1)] + near(0) + [self.a_far]
                + near(3) + near(1) + [lambda: self.b_far(0)] + near(2)
                + [lambda: self.b_far(3), lambda: self.b_far(1), lambda: self.b_far(2)])

    def settle(self):
        ref = self.buf.at[pl.ds(0, 16 * self.rows), pl.ds(self.col, self.cols)]
        pltpu.make_async_copy(ref, ref, self.twin[1]).wait()

    def drain(self):
        ref = self.buf.at[pl.ds(0, 15 * self.rows), pl.ds(self.col, self.cols)]
        pltpu.make_async_copy(ref, ref, self.send).wait()
        if self.twin is not None:
            ref = self.buf.at[pl.ds(0, 16 * self.rows), pl.ds(self.col, self.cols)]
            pltpu.make_async_copy(ref, ref, self.twin[0]).wait()


def col_halves(cols, rows, flip):
    lo = cols // 256 * 128
    if flip:
        lo = cols - lo
    return ((0, rows, 0, lo), (0, rows, lo, cols - lo))


PIECES = ((0, 128, "xz"), (128, 256, "zx"), (384, 384, "xz"), (768, 640, "zx"), (1408, 512, "xz"), (1920, 1024, "zx"))
PEERS = ((1, 0, 0), (-1, 0, 0), (2, 0, 0), (0, 1, 0), (0, -1, 0), (0, 2, 0), (0, 0, 1), (0, 0, -1), (0, 0, 2), (0, 0, -2),
         (0, 0, 4), (0, 0, -4), (0, 0, 8), (0, 0, 0, 1))


def nt(a, b):
    return lax.dot_general(a, b, (((1,), (1,)), ((), ())), preferred_element_type=F32)


def tn(a, b):
    return lax.dot_general(a, b, (((0,), (0,)), ((), ())), preferred_element_type=F32)


def gather_phase(act, gain, wq, wk, wv, wo, cot, wall, kv, normed, rs, q, g, sends, recvs, twins, ksend, krecv):
    barrier = pltpu.get_barrier_semaphore()
    for p in PEERS:
        pl.semaphore_signal(barrier, inc=1, device_id=dev(*p), device_id_type=MESH)
    x, y, z, c = spot()
    mine = pl.ds(pl.multiple_of(((x * 4 + lax.rem(z, 4)) * 2 + c) * SHARD, 16), SHARD)
    wall[mine, 0:128] = wk[...]
    wall[mine, 256:384] = jnp.zeros((SHARD, 128), BF)
    wall[mine, 128:320] = wv[...]
    wall[mine, 384:1408] = wq[...]
    wall[mine, 1408:2944] = wo[...]
    pl.semaphore_wait(barrier, len(PEERS))

    def row(order):
        def of(ka, kb):
            kx, kz = (ka, kb) if order == "xz" else (kb, ka)
            return ((lax.rem(x + kx, 4) * 4 + lax.rem(z + kz, 4)) * 2 + c) * SHARD
        return of

    parts = [Gather(wall, row(o), SHARD, c0, nc, col_halves(nc, SHARD, i % 2), o, sends.at[i], recvs, 20 * i,
                    (twins.at[0, i], twins.at[1, i])) for i, (c0, nc, o) in enumerate(PIECES)]

    def run(group):
        for line in zip(*[p.steps() for p in group]):
            for s in line:
                s()

    a = parts[0].steps(), parts[1].steps()
    for i in range(3):
        a[0][i](); a[1][i]()
    for p in parts[2:]:
        p.first()
    wide = act[...].astype(F32)
    r = lax.rsqrt(jnp.mean(wide * wide, axis=-1, keepdims=True) + 1e-6)
    rs[...] = r
    normed[...] = (wide * r * gain[...]).astype(BF)
    for i in range(3, len(a[0])):
        a[0][i](); a[1][i]()
    parts[0].settle(); parts[1].settle()
    both = jnp.dot(normed[...], wall[:, 0:320], preferred_element_type=F32).astype(BF)
    own = pl.ds(pl.multiple_of((lax.div(z, 4) * 4 + y) * 128, 128), 128)
    kv[own, 256:384] = jnp.zeros((128, 128), BF)
    kv[own, 0:320] = both

    def kv_row(ka, kb):
        return (lax.rem(lax.div(z, 4) + ka, 4) * 4 + lax.rem(y + kb, 4)) * 128

    kvg = Gather(kv, kv_row, 128, 0, 384, ((0, 64, 0, 384), (64, 64, 0, 384)), "wy", ksend, krecv, 0)
    ks = kvg.steps()
    bulk = [p.steps()[1:] for p in parts[2:]]
    ks[0]()
    for i in range(len(bulk[0])):
        for b in bulk:
            b[i]()
        ks[i + 1]()
    parts[2].settle(); parts[3].settle()
    qs = (jnp.dot(normed[...], wall[:, 384:1408], preferred_element_type=F32) * HQ ** -0.5).astype(BF)
    for h in range(HEADS):
        q[pl.ds(h * 128, 128), :] = qs[:, h * HQ:(h + 1) * HQ]
    parts[4].settle(); parts[5].settle()
    for h in range(HEADS):
        g[pl.ds(h * 128, 128), :] = nt(cot[...], wall[pl.ds(h * DV, DV), 1408:2944]).astype(BF)
    for p in parts:
        p.drain()
    kvg.drain()


def softmax_phase(q, g, kv, e, vt, gt, att, inv, centre):
    vt[...] = kv[:, 128:320].T
    gt[...] = g[...].T
    wide = 512

    @pl.loop(0, 1024 // wide)
    def _(i):
        at = pl.ds(pl.multiple_of(i * wide, wide), wide)
        s = nt(kv[:, 0:128], q[at, :])
        p = jnp.exp(s - jnp.max(s, axis=0, keepdims=True))
        r = 1.0 / jnp.sum(p, axis=0, keepdims=True)
        pb = p.astype(BF)
        e[:, at] = pb
        a = jnp.dot(vt[...], pb, preferred_element_type=F32) * r
        att[:, at] = a.astype(BF)
        inv[:, at] = r
        centre[:, at] = jnp.sum(a * gt[:, at].astype(F32), axis=0, keepdims=True)


def grads_of(rows, q, g, kv, e, inv, centre, part, dqt, start):
    dp = nt(kv[rows, 128:320], g[...])
    p = e[rows, :].astype(F32) * inv[...]
    part[rows, 128:320] = jnp.dot(p.astype(BF), g[...], preferred_element_type=F32).astype(BF)
    ds = (p * (dp - centre[...])).astype(BF)
    part[rows, 0:128] = jnp.dot(ds, q[...], preferred_element_type=F32).astype(BF)
    term = tn(kv[rows, 0:128], ds)
    if start:
        dqt[...] = term
    else:
        dqt[...] += term


def body(act, gain, wq, wk, wv, wo, cot, out, ingrad, wgrad,
         wall, kv, normed, rs, q, g, e, vt, gt, att, inv, centre, part, dqt, rows_of, ng,
         ybuf, zsend, zbuf, wg, cbuf, xs, xbuf, ys, ybuf2, zs, zbuf2, hs, hbuf, last,
         sends, recvs, twins, ksend, krecv, ysem, zsem, wsem):
    part[:, 256:384] = jnp.zeros((2048, 128), BF)
    gather_phase(act, gain, wq, wk, wv, wo, cot, wall, kv, normed, rs, q, g, sends, recvs, twins, ksend, krecv)
    softmax_phase(q, g, kv, e, vt, gt, att, inv, centre)
    x, y, z, c = spot()
    zh, zl = lax.div(z, 4), lax.rem(z, 4)
    wide = lambda ref: ref.astype(F32)

    def send(src, dst, sems, to):
        cp = pltpu.make_async_remote_copy(src_ref=src, dst_ref=dst, send_sem=sems.at[0], recv_sem=sems.at[1],
                                          device_id=to, device_id_type=MESH)
        cp.start()
        return cp

    def group(k):
        return lax.rem(zh + k, 4) * 512

    def block(k, dy):
        return pl.ds(pl.multiple_of(group(k) + lax.rem(y + dy, 4) * 128, 128), 128)

    yc, zc = {}, {}

    def out_y(k):
        yc[k] = [send(part.at[block(k, dy)], ybuf.at[k, dy - 1], ysem.at[k, dy - 1], dev(0, dy)) for dy in (1, 3, 2)]

    def out_z(k):
        for cp in yc[k]:
            cp.wait()
        zsend[k] = (wide(part[block(k, 0), :]) + wide(ybuf[k, 0]) + wide(ybuf[k, 1]) + wide(ybuf[k, 2])).astype(BF)
        if k:
            zc[k] = send(zsend.at[k], zbuf.at[k - 1], zsem.at[k - 1], dev(0, 0, 4 * k))

    previous = None
    for k in (2, 1, 3, 0):
        grads_of(pl.ds(pl.multiple_of(group(k), 512), 512), q, g, kv, e, inv, centre, part, dqt, k == 2)
        out_y(k)
        if previous is not None:
            out_z(previous)
        previous = k
    for h in range(HEADS):
        rows_of[:, h * HQ:(h + 1) * HQ] = (dqt[:, h * 128:(h + 1) * 128].T * HQ ** -0.5).astype(BF)
    ng[...] = nt(rows_of[:, 0:1024], wall[:, 384:1408])
    out_z(0)
    for k in (1, 2, 3):
        zc[k].wait()
    kvg = (wide(zsend[0]) + wide(zbuf[0]) + wide(zbuf[1]) + wide(zbuf[2])).astype(BF)

    wg[...] = tn(normed[...], kvg).astype(BF).reshape(4, 4, 2, SHARD, 384)
    cp = send(wg.at[:, :, 1 - c], cbuf, wsem.at[0], dev(0, 0, 0, 1))
    scaled = (ng[...] + nt(kvg[:, 0:320], wall[:, 0:320])) * gain[...]
    cp.wait()
    xs[...] = (wide(wg[:, :, c]) + wide(cbuf[...])).astype(BF)
    cps = [send(xs.at[lax.rem(x + d, 4)], xbuf.at[d - 1], wsem.at[d], dev(d)) for d in (1, 3, 2)]
    a, r = wide(act[...]), rs[...]
    inner = jnp.mean(scaled * a, axis=-1, keepdims=True)
    ingrad[...] = (wide(cot[...]) + r * (scaled - a * r * r * inner)).astype(BF)
    for h in range(0, HEADS, 2):
        pair = att[:, h * 128:(h + 2) * 128].T
        rows_of[:, h * DV:(h + 2) * DV] = jnp.concatenate([pair[:128], pair[128:]], axis=1)
    for cp in cps:
        cp.wait()
    ys[...] = (wide(xs[x]) + wide(xbuf[0]) + wide(xbuf[1]) + wide(xbuf[2])).astype(BF)
    cps = [send(ys.at[lax.rem(y + d, 4)], ybuf2.at[d - 1], wsem.at[3 + d], dev(0, d)) for d in (1, 3, 2)]
    half = 768
    out[:, 0:half] = (wide(act[:, 0:half]) + jnp.dot(rows_of[...], wall[:, 1408:1408 + half], preferred_element_type=F32)).astype(BF)
    for cp in cps:
        cp.wait()
    zs[...] = (wide(ys[y]) + wide(ybuf2[0]) + wide(ybuf2[1]) + wide(ybuf2[2])).astype(BF)
    turn = lax.rem(y - zl + 4, 4)
    for t in (1, 2, 3):
        @pl.when(turn == t)
        def _():
            send(zs, zbuf2.at[t - 1], wsem.at[6 + t], dev(0, 0, t if t < 3 else -1)).wait_send()
    out[:, half:] = (wide(act[:, half:]) + jnp.dot(rows_of[...], wall[:, 1408 + half:], preferred_element_type=F32)).astype(BF)

    @pl.when(turn == 0)
    def _():
        for t in (1, 2, 3):
            pltpu.make_async_copy(zs, zbuf2.at[t - 1], wsem.at[6 + t, 1]).wait()
        hs[...] = (wide(zs[...]) + wide(zbuf2[0]) + wide(zbuf2[1]) + wide(zbuf2[2])).astype(BF)
        for cp in [send(hs, hbuf.at[k - 1], wsem.at[9 + k], dev(0, 0, 4 * k)) for k in (2, 1, 3)]:
            cp.wait()
        last[...] = (wide(hs[...]) + wide(hbuf[0]) + wide(hbuf[1]) + wide(hbuf[2])).astype(BF)
        for cp in [send(last, last, wsem.at[12 + d], dev(0, d)) for d in (1, 3, 2)]:
            cp.wait_send()

    for d in (1, 2, 3):
        @pl.when(lax.rem(zl + d, 4) == y)
        def _():
            pltpu.make_async_copy(last, last, wsem.at[12 + d, 1]).wait()
    wgrad[...] = wide(last[:, 0:320])


def per_device(act, gain, wq, wk, wv, wo, cot):
    vm = pl.BlockSpec(memory_space=pltpu.VMEM)
    V, DMA = pltpu.VMEM, pltpu.SemaphoreType.DMA
    scratch = [
        V((1536, COLS), BF), V((2048, 384), BF), V((128, 1536), BF), V((128, 1), F32), V((1024, 128), BF), V((1024, 192), BF),
        V((2048, 1024), BF), V((192, 2048), BF), V((192, 1024), BF), V((192, 1024), BF), V((1, 1024), F32), V((1, 1024), F32),
        V((2048, 384), BF), V((128, 1024), F32), V((128, 1536), BF), V((128, 1536), F32),
        V((4, 3, 128, 384), BF), V((4, 128, 384), BF), V((3, 128, 384), BF), V((4, 4, 2, SHARD, 384), BF),
        V((4, 4, SHARD, 384), BF), V((4, 4, SHARD, 384), BF), V((3, 4, SHARD, 384), BF), V((4, SHARD, 384), BF),
        V((3, SHARD, 384), BF), V((SHARD, 384), BF), V((3, SHARD, 384), BF), V((SHARD, 384), BF), V((3, SHARD, 384), BF),
        V((SHARD, 384), BF),
        DMA((6,)), DMA((120,)), DMA((2, 6)), DMA, DMA((20,)), DMA((4, 3, 2)), DMA((3, 2)), DMA((16, 2)),
    ]
    o, i, w = pl.pallas_call(
        body,
        out_shape=(jax.ShapeDtypeStruct((128, 1536), BF), jax.ShapeDtypeStruct((128, 1536), BF),
                   jax.ShapeDtypeStruct((SHARD, 320), F32)),
        in_specs=[vm] * 7, out_specs=(vm,) * 3, scratch_shapes=scratch,
        compiler_params=pltpu.CompilerParams(collective_id=0, has_side_effects=True, vmem_limit_bytes=58 * 2**20),
        name="layer",
    )(act[0], gain.reshape(1, -1), wq, wk, wv, wo, cot[0])
    return o[None], i[None], w


def solution(mesh):
    rows = P("dp", "seq", None)
    split = P("dp", None)
    return jax.shard_map(per_device, mesh=mesh, in_specs=(rows, P(), split, split, split, split, rows),
                         out_specs=(rows, rows, split), check_vma=False)
```

```python
import functools
import jax
import jax.numpy as jnp
from jax import lax
from jax.experimental import pallas as pl
from jax.experimental.pallas import tpu as pltpu
from jax.sharding import PartitionSpec as P

MESH = pl.DeviceIdType.MESH
BF = jnp.bfloat16
F32 = jnp.float32
HEADS, HQ, DV = 8, 128, 192
COLS = 2944
SHARD = 48


def spot():
    dp, sq = lax.axis_index("dp"), lax.axis_index("seq")
    x, zl, c = lax.div(dp, 8), lax.div(lax.rem(dp, 8), 2), lax.rem(dp, 2)
    zh, y = lax.div(sq, 4), lax.rem(sq, 4)
    return x, y, zh * 4 + zl, c


def dev(dx=0, dy=0, dz=0, dc=0):
    x, y, z, c = spot()
    x, y = lax.rem(x + dx + 4, 4), lax.rem(y + dy + 4, 4)
    z, c = lax.rem(z + dz + 16, 16), lax.rem(c + dc, 2)
    return (x * 8 + lax.rem(z, 4) * 2 + c, lax.div(z, 4) * 4 + y)


AXES = {
    "x": ((1, 0, 0), (-1, 0, 0)),
    "y": ((0, 1, 0), (0, -1, 0)),
    "z": ((0, 0, 1), (0, 0, -1)),
}


class Gather:
    def __init__(self, buf, row_of, rows, col, cols, halves, order, send, recv, base, twin=None, direct=False):
        self.buf, self.row_of, self.rows, self.col, self.cols = buf, row_of, rows, col, cols
        self.halves, self.order, self.send, self.recv, self.base = halves, order, send, recv, base
        self.twin, self.direct = twin, direct

    def block(self, ka, kb, part=None):
        r0, nr, c0, nc = part if part else (0, self.rows, 0, self.cols)
        return self.buf.at[pl.ds(pl.multiple_of(self.row_of(ka, kb) + r0, 16), nr), pl.ds(self.col + c0, nc)]

    def copy(self, ka, kb, part, to, slot):
        ref = self.block(ka, kb, part)
        return pltpu.make_async_remote_copy(
            src_ref=ref, dst_ref=ref, send_sem=self.send, recv_sem=self.recv.at[self.base + slot],
            device_id=to, device_id_type=MESH)

    def put(self, ka, kb, part, axis, way, slot):
        if part is not None and (part[1] == 0 or part[3] == 0):
            return
        self.copy(ka, kb, part, dev(*AXES[self.order[axis]][way]), slot).start()

    def far(self, k, axis, slot):
        if self.direct:
            self.copy(k, 0, None, dev(*[2 * d for d in AXES[self.order[axis]][0]]), slot).start()

    def got(self, ka, kb, part, slot):
        if part is not None and (part[1] == 0 or part[3] == 0):
            return
        self.copy(ka, kb, part, dev(*AXES[self.order[0]][0]), slot).wait_recv()

    def share(self, ka, kb):
        if self.twin is None:
            return
        ref = self.block(ka, kb)
        pltpu.make_async_remote_copy(
            src_ref=ref, dst_ref=ref, send_sem=self.twin[0], recv_sem=self.twin[1],
            device_id=dev(0, 0, 0, 1), device_id_type=MESH).start()

    def first(self):
        self.put(0, 0, None, 0, 0, 0)
        self.put(0, 0, None, 0, 1, 1)
        self.far(0, 0, 2)
        self.second(0)
        self.share(0, 0)

    def second(self, k):
        self.put(k, 0, None, 1, 0, 4 + 4 * k)
        self.put(k, 0, None, 1, 1, 5 + 4 * k)
        self.far(k, 1, 6 + 4 * k)

    def a_near(self, k, way):
        self.got(k, 0, None, 0 if k == 3 else 1)
        if not self.direct:
            self.put(k, 0, self.halves[way], 0, way, 2 + way)
        self.second(k)
        self.share(k, 0)

    def a_far(self):
        if self.direct:
            self.got(2, 0, None, 2)
        else:
            self.got(2, 0, self.halves[0], 2)
            self.got(2, 0, self.halves[1], 3)
        self.second(2)
        self.share(2, 0)

    def b_near(self, k, kb, way):
        self.got(k, kb, None, 4 + 4 * k + (0 if kb == 3 else 1))
        if not self.direct:
            self.put(k, kb, self.halves[way], 1, way, 6 + 4 * k + way)
        self.share(k, kb)

    def b_far(self, k):
        if self.direct:
            self.got(k, 2, None, 6 + 4 * k)
        else:
            self.got(k, 2, self.halves[0], 6 + 4 * k)
            self.got(k, 2, self.halves[1], 7 + 4 * k)
        self.share(k, 2)

    def steps(self):
        near = lambda k: [lambda: self.b_near(k, 3, 0), lambda: self.b_near(k, 1, 1)]
        return ([self.first, lambda: self.a_near(3, 0), lambda: self.a_near(1, 1)] + near(0) + [self.a_far]
                + near(3) + near(1) + [lambda: self.b_far(0)] + near(2)
                + [lambda: self.b_far(3), lambda: self.b_far(1), lambda: self.b_far(2)])

    def settle(self):
        ref = self.buf.at[pl.ds(0, 16 * self.rows), pl.ds(self.col, self.cols)]
        pltpu.make_async_copy(ref, ref, self.twin[1]).wait()

    def drain(self):
        ref = self.buf.at[pl.ds(0, 15 * self.rows), pl.ds(self.col, self.cols)]
        pltpu.make_async_copy(ref, ref, self.send).wait()
        if self.twin is not None:
            ref = self.buf.at[pl.ds(0, 16 * self.rows), pl.ds(self.col, self.cols)]
            pltpu.make_async_copy(ref, ref, self.twin[0]).wait()


def col_halves(cols, rows, flip):
    lo = cols // 256 * 128
    if flip:
        lo = cols - lo
    return ((0, rows, 0, lo), (0, rows, lo, cols - lo))


PIECES = ((0, 128, "xz"), (128, 256, "zx"), (384, 384, "xz"), (768, 640, "zx"), (1408, 512, "xz"), (1920, 1024, "zx"))
PLANE = [(dx, 0, dz) for dx in (0, 1, -1, 2) for dz in (0, 1, -1, 2)][1:]
PEERS = [(2, 0, -2), (1, 0, -2), (-1, 0, -2), (0, 0, -2)] + PLANE + [
    (0, 1, 0), (0, -1, 0), (0, 2, 0), (0, 0, 4), (0, 0, -4), (0, 0, 8), (0, 0, 0, 1)]


def nt(a, b):
    return lax.dot_general(a, b, (((1,), (1,)), ((), ())), preferred_element_type=F32)


def tn(a, b):
    return lax.dot_general(a, b, (((0,), (0,)), ((), ())), preferred_element_type=F32)


def hello():
    barrier = pltpu.get_barrier_semaphore()
    for p in PEERS:
        pl.semaphore_signal(barrier, inc=1, device_id=dev(*p), device_id_type=MESH)
    return barrier


def remote(src, dst, send, recv, to):
    return pltpu.make_async_remote_copy(src_ref=src, dst_ref=dst, send_sem=send, recv_sem=recv, device_id=to,
                                        device_id_type=MESH)


def pack(v):
    return jnp.concatenate([v[..., :64, :], v[..., 64:, :]], axis=-1)


def unpack(w):
    return jnp.concatenate([w[..., :64], w[..., 64:]], axis=-2)


class Window:
    def __init__(self, buf, sends, recvs):
        self.buf, self.sends, self.recvs = buf, sends, recvs

    def at(self, kz, half=None):
        x, y, z, c = spot()
        b = self.buf.at[lax.rem(lax.div(z, 4) + kz, 4) * 4 + y]
        return b if half is None else b.at[pl.ds(160 * half, 160)]

    def hop(self, kz, half, up, slot):
        ref = self.at(kz, half)
        return remote(ref, ref, self.sends.at[slot], self.recvs.at[slot], dev(0, 0, 4 if up else -4))

    def across(self, kz, half, dy):
        ref, slot = self.at(kz, half), 6 + (kz * 2 + half) * 3 + dy - 1
        return remote(ref, ref, self.sends.at[slot], self.recvs.at[slot], dev(0, dy))

    def row(self, kz, half):
        for dy in (1, 3, 2):
            self.across(kz, half, dy).start()

    def got(self, kz, half, slot):
        self.hop(kz, half, True, slot).wait_recv()

    def steps(self):
        def s0():
            self.hop(0, 0, True, 0).start()
            self.hop(0, 1, False, 1).start()
            self.hop(0, 1, True, 2).start()
            self.hop(0, 0, False, 3).start()
            self.row(0, 0)
            self.row(0, 1)

        def s1():
            self.got(3, 0, 0)
            self.hop(3, 0, True, 4).start()
            self.row(3, 0)

        def s2():
            self.got(1, 1, 1)
            self.hop(1, 1, False, 5).start()
            self.row(1, 1)

        def s3():
            self.got(3, 1, 2)
            self.row(3, 1)

        def s4():
            self.got(1, 0, 3)
            self.row(1, 0)

        def s5():
            self.got(2, 0, 4)
            self.row(2, 0)
            self.got(2, 1, 5)
            self.row(2, 1)

        def s6():
            for kz, half in ((0, 0), (0, 1), (3, 0), (1, 1), (3, 1), (1, 0), (2, 0), (2, 1)):
                for dy in (1, 3, 2):
                    self.across(kz, half, dy).wait_recv()

        return [s0, s1, s2, s3, s4, s5, s6]

    def drain(self):
        for slot in range(30):
            ref = self.at(0, 0)
            remote(ref, ref, self.sends.at[slot], self.recvs.at[slot], dev(0, 1)).wait_send()


def gather_phase(act, gain, wq, wk, wv, wo, cot, wall, kvp, normed, rs, q, sends, recvs, twins, ksend, krecv):
    barrier = hello()
    x, y, z, c = spot()
    mine = pl.ds(pl.multiple_of(((x * 4 + lax.rem(z, 4)) * 2 + c) * SHARD, 16), SHARD)
    wall[mine, 0:128] = wk[...]
    wall[mine, 256:384] = jnp.zeros((SHARD, 128), BF)
    wall[mine, 128:320] = wv[...]
    wall[mine, 384:1408] = wq[...]
    wall[mine, 1408:2944] = wo[...]
    wide = act[...].astype(F32)
    r = lax.rsqrt(jnp.mean(wide * wide, axis=-1, keepdims=True) + 1e-6)
    rs[...] = r
    normed[...] = (wide * r * gain[...][None, :]).astype(BF)
    pl.semaphore_wait(barrier, len(PEERS))

    def row(order):
        def of(ka, kb):
            kx, kz = (ka, kb) if order == "xz" else (kb, ka)
            return ((lax.rem(x + kx, 4) * 4 + lax.rem(z + kz, 4)) * 2 + c) * SHARD
        return of

    parts = [Gather(wall, row(o), SHARD, c0, nc, col_halves(nc, SHARD, i % 2), o, sends.at[i], recvs, 20 * i,
                    (twins.at[0, i], twins.at[1, i]), i < 2) for i, (c0, nc, o) in enumerate(PIECES)]
    kvs = [p.steps() for p in parts[:2]]
    bulk = [p.steps() for p in parts[2:]]

    def do(group, i):
        for steps in group:
            steps[i]()

    do(kvs, 0)
    for i in (1, 2, 5):
        do(kvs, i)
    do(bulk, 0)
    for i in (3, 4, 6, 7, 8, 9, 10, 11, 12, 13, 14, 15):
        do(kvs, i)
    parts[0].settle(); parts[1].settle()
    both = jnp.dot(normed[...], wall[:, 0:320], preferred_element_type=F32).astype(BF)
    own = lax.div(z, 4) * 4 + y
    kvp[own, 0:128, :] = both[:, 0:128]
    kvp[own, 128:256, :] = both[:, 128:256]
    kvp[own, 256:320, :] = pack(both[:, 256:320])
    win = Window(kvp, ksend, krecv)
    ks = win.steps()
    ks[0]()
    do(bulk, 1); do(bulk, 2); do(bulk, 3); do(bulk, 4); do(bulk, 5)
    ks[1](); ks[2]()
    do(bulk, 6); do(bulk, 7)
    ks[3](); ks[4]()
    do(bulk, 8); do(bulk, 9); do(bulk, 10)
    ks[5]()
    do(bulk, 11); do(bulk, 12); do(bulk, 13); do(bulk, 14); do(bulk, 15)
    parts[2].settle(); parts[3].settle()
    qs = (jnp.dot(normed[...], wall[:, 384:1408], preferred_element_type=F32) * HQ ** -0.5).astype(BF)
    for h in range(HEADS):
        q[pl.ds(h * 128, 128), :] = qs[:, h * HQ:(h + 1) * HQ]
    ks[6]()

    def finish():
        parts[4].settle(); parts[5].settle()
        for p in parts:
            p.drain()
        win.drain()
    return finish


def keys_of(kvp, first, n):
    return kvp[pl.ds(first, n), 0:128, :].reshape(n * 128, 128)


def softmax_phase(q, kvp, v, e, vt, att, inv):
    v[:, 0:128] = kvp[:, 128:256, :].reshape(2048, 128)
    v[:, 128:192] = unpack(kvp[:, 256:320, :]).reshape(2048, 64)
    vt[...] = v[...].T
    wide = 512

    @pl.loop(0, 1024 // wide)
    def _(i):
        at = pl.ds(pl.multiple_of(i * wide, wide), wide)
        s = nt(keys_of(kvp, 0, 16), q[at, :])
        p = jnp.exp(s - jnp.max(s, axis=0, keepdims=True))
        r = 1.0 / jnp.sum(p, axis=0, keepdims=True)
        pb = p.astype(BF)
        e[:, at] = pb
        att[:, at] = jnp.dot(vt[...], pb, preferred_element_type=F32) * r
        inv[:, at] = r


def value_terms(first, g, e, inv, part):
    rows = pl.ds(pl.multiple_of(first * 128, 512), 512)
    p = (e[rows, :].astype(F32) * inv[...]).astype(BF)
    dv = jnp.dot(p, g[...], preferred_element_type=F32).astype(BF).reshape(4, 128, 192)
    part[pl.ds(first, 4), 0:128, :] = dv[:, :, 0:128]
    part[pl.ds(first, 4), 128:192, :] = pack(dv[:, :, 128:192])


def key_terms(first, q, g, kvp, v, e, inv, centre, part, dqt, start):
    rows = pl.ds(pl.multiple_of(first * 128, 512), 512)
    dp = nt(v[rows, :], g[...])
    ds = (e[rows, :].astype(F32) * inv[...] * (dp - centre[...])).astype(BF)
    part[pl.ds(first, 4)] = jnp.dot(ds, q[...], preferred_element_type=F32).astype(BF).reshape(4, 128, 128)
    term = tn(keys_of(kvp, first, 4), ds)
    if start:
        dqt[...] = term
    else:
        dqt[...] += term


def post(src, dst, sems, to):
    cp = remote(src, dst, sems.at[0], sems.at[1], to)
    cp.start()
    return cp


class Total:
    def __init__(self, part, ybuf, zs, mid, fbuf, zbuf, wg, cbuf, xs, xbuf, ps, pbuf, hs, hbuf, sems):
        self.part, self.ybuf, self.zs, self.mid, self.fbuf, self.zbuf = part, ybuf, zs, mid, fbuf, zbuf
        self.wg, self.cbuf, self.xs, self.xbuf, self.ps, self.pbuf = wg, cbuf, xs, xbuf, ps, pbuf
        self.hs, self.hbuf, self.sems = hs, hbuf, sems
        self.rows = part.shape[1]
        self.x, self.y, self.z, self.c = spot()
        self.zh, self.zl = lax.div(self.z, 4), lax.rem(self.z, 4)
        self.yc, self.zc = {}, []

    def group(self, k):
        return lax.rem(self.zh + k, 4) * 4

    def y_out(self, k):
        self.yc[k] = [post(self.part.at[self.group(k) + lax.rem(self.y + dy, 4)], self.ybuf.at[k, dy - 1],
                           self.sems.at[k * 3 + dy - 1], dev(0, dy)) for dy in (1, 3, 2)]

    def y_in(self, k):
        for cp in self.yc[k]:
            cp.wait()
        f = lambda t: t.astype(F32)
        self.zs[k] = (f(self.part[self.group(k) + self.y]) + f(self.ybuf[k, 0]) + f(self.ybuf[k, 1]) + f(self.ybuf[k, 2])).astype(BF)
        half = self.rows // 2
        low, high = pl.ds(0, half), pl.ds(half, half)
        if k == 2:
            self.fc = [post(self.zs.at[2, low], self.fbuf.at[0], self.sems.at[12], dev(0, 0, 4)),
                       post(self.zs.at[2, high], self.fbuf.at[1], self.sems.at[13], dev(0, 0, -4))]
        if k == 1:
            self.zc.append(post(self.zs.at[1, high], self.zbuf.at[0, high], self.sems.at[14], dev(0, 0, 4)))
        if k == 3:
            self.zc.append(post(self.zs.at[3, low], self.zbuf.at[1, low], self.sems.at[15], dev(0, 0, -4)))

    def z_mid(self, way):
        half = self.rows // 2
        rows = pl.ds(half * way, half)
        self.fc[way].wait()
        self.mid[way] = (self.zs[3 if way else 1, rows].astype(F32) + self.fbuf[way].astype(F32)).astype(BF)
        self.zc.append(post(self.mid.at[way], self.zbuf.at[way, rows], self.sems.at[16 + way], dev(0, 0, -4 if way else 4)))

    def z_in(self):
        for cp in self.zc:
            cp.wait()
        return (self.zs[0].astype(F32) + self.zbuf[0].astype(F32) + self.zbuf[1].astype(F32)).astype(BF)

    def t0(self, normed, grad):
        self.wg[...] = tn(normed[...], grad).astype(BF).reshape(self.wg.shape)
        self.cps = [post(self.wg.at[:, :, 1 - self.c], self.cbuf, self.sems.at[18], dev(0, 0, 0, 1))]

    def wait(self):
        for cp in self.cps:
            cp.wait()

    def t1(self):
        self.wait()
        self.xs[...] = (self.wg[:, :, self.c].astype(F32) + self.cbuf[...].astype(F32)).astype(BF)
        self.cps = [post(self.xs.at[lax.rem(self.x + dx + 4, 4), lax.rem(self.zl + dz + 4, 4)], self.xbuf.at[i],
                         self.sems.at[19 + i], dev(dx, 0, dz)) for i, (dx, _, dz) in enumerate(PLANE)]

    def t2(self):
        self.wait()
        total = self.xs[self.x, self.zl].astype(F32)
        for i in range(15):
            total += self.xbuf[i].astype(F32)
        self.ps[...] = total.astype(BF)
        self.cps = [post(self.ps, self.pbuf.at[k - 1], self.sems.at[33 + k], dev(0, 0, 4 * k)) for k in (2, 1, 3)]

    def t3(self):
        self.wait()
        self.hs[...] = in_order(self.ps, self.pbuf, self.zh).astype(BF)
        self.cps = [post(self.hs, self.hbuf.at[d - 1], self.sems.at[36 + d], dev(0, d)) for d in (1, 3, 2)]

    def t4(self):
        self.wait()
        return in_order(self.hs, self.hbuf, self.y)


def in_order(mine, others, place):
    total = None
    for i in range(4):
        d = lax.rem(place - i + 4, 4)
        term = mine[...].astype(F32)
        for j in (1, 2, 3):
            term = jnp.where(d == j, others[j - 1].astype(F32), term)
        total = term if total is None else total + term
    return total


def body(act, gain, wq, wk, wv, wo, cot, out, ingrad, wgrad,
         wall, kvp, normed, rs, q, g, v, e, vt, att, inv, centre, dqt, rows_of, ng,
         sends, recvs, twins, ksend, krecv, *slabs):
    finish = gather_phase(act, gain, wq, wk, wv, wo, cot, wall, kvp, normed, rs, q, sends, recvs, twins, ksend, krecv)
    softmax_phase(q, kvp, v, e, vt, att, inv)
    finish()
    for h in range(HEADS):
        g[pl.ds(h * 128, 128), :] = nt(cot[...], wall[pl.ds(h * DV, DV), 1408:2944]).astype(BF)
    half = len(slabs) // 2
    K, V = Total(*slabs[:half]), Total(*slabs[half:])

    for k in (2, 1, 3, 0):
        value_terms(V.group(k), g, e, inv, V.part)
        V.y_out(k)
    centre[...] = jnp.sum(att[...] * g[...].astype(F32).T, axis=0, keepdims=True)
    for k in (2, 1, 3, 0):
        key_terms(K.group(k), q, g, kvp, v, e, inv, centre, K.part, dqt, k == 2)
        K.y_out(k)
        if k != 0:
            V.y_in(k)
    for h in range(HEADS):
        rows_of[:, h * HQ:(h + 1) * HQ] = (dqt[:, h * 128:(h + 1) * 128].T * HQ ** -0.5).astype(BF)
    ng[...] = nt(rows_of[:, 0:1024], wall[:, 384:1408])
    V.z_mid(0)
    V.z_mid(1)
    V.y_in(0)
    K.y_in(2)
    K.y_in(1)
    K.y_in(3)
    vsum = V.z_in()
    vgrad = jnp.concatenate([vsum[0:128], unpack(vsum[128:192])], axis=1)
    V.t0(normed, jnp.concatenate([vgrad, jnp.zeros((128, 64), BF)], axis=1))
    K.z_mid(0)
    K.z_mid(1)
    V.t1()
    K.y_in(0)
    kgrad = K.z_in()
    K.t0(normed, kgrad)
    scaled = (ng[...] + nt(jnp.concatenate([kgrad, vgrad], axis=1), wall[:, 0:320])) * gain[...][None, :]
    K.t1()
    a, r = act[...].astype(F32), rs[...]
    inner = jnp.mean(scaled * a, axis=-1, keepdims=True)
    ingrad[...] = (cot[...].astype(F32) + r * (scaled - a * r * r * inner)).astype(BF)
    V.t2()
    for h in range(0, HEADS, 2):
        pair = att[:, h * 128:(h + 2) * 128].T.astype(BF)
        rows_of[:, h * DV:(h + 2) * DV] = jnp.concatenate([pair[:128], pair[128:]], axis=1)
    out[...] = (a + jnp.dot(rows_of[...], wall[:, 1408:2944], preferred_element_type=F32)).astype(BF)
    K.t2()
    V.t3()
    K.t3()
    wgrad[:, 128:320] = V.t4()[:, 0:192]
    wgrad[:, 0:128] = K.t4()


def per_device(act, gain, wq, wk, wv, wo, cot):
    vm = pl.BlockSpec(memory_space=pltpu.VMEM)
    V, DMA = pltpu.VMEM, pltpu.SemaphoreType.DMA
    def slab(rows, cols):
        return [V((16, rows, 128), BF), V((4, 3, rows, 128), BF), V((4, rows, 128), BF), V((2, rows // 2, 128), BF),
                V((2, rows // 2, 128), BF), V((2, rows, 128), BF), V((4, 4, 2, SHARD, cols), BF), V((4, 4, SHARD, cols), BF),
                V((4, 4, SHARD, cols), BF), V((15, SHARD, cols), BF), V((SHARD, cols), BF), V((3, SHARD, cols), BF),
                V((SHARD, cols), BF), V((3, SHARD, cols), BF), DMA((40, 2))]

    scratch = [
        V((1536, COLS), BF), V((16, 320, 128), BF), V((128, 1536), BF), V((128, 1), F32), V((1024, 128), BF), V((1024, 192), BF),
        V((2048, 192), BF), V((2048, 1024), BF), V((192, 2048), BF), V((192, 1024), F32), V((1, 1024), F32), V((1, 1024), F32),
        V((128, 1024), F32), V((128, 1536), BF), V((128, 1536), F32),
        DMA((6,)), DMA((120,)), DMA((2, 6)), DMA((30,)), DMA((30,)),
    ] + slab(128, 128) + slab(192, 256)
    o, i, w = pl.pallas_call(
        body,
        out_shape=(jax.ShapeDtypeStruct((128, 1536), BF), jax.ShapeDtypeStruct((128, 1536), BF),
                   jax.ShapeDtypeStruct((SHARD, 320), F32)),
        in_specs=[vm] * 7, out_specs=(vm,) * 3, scratch_shapes=scratch,
        compiler_params=pltpu.CompilerParams(collective_id=0, has_side_effects=True, vmem_limit_bytes=58 * 2**20),
        name="layer",
    )(act[0], gain, wq, wk, wv, wo, cot[0])
    return o[None], i[None], w


def solution(mesh):
    rows = P("dp", "seq", None)
    split = P("dp", None)
    return jax.shard_map(per_device, mesh=mesh, in_specs=(rows, P(), split, split, split, split, rows),
                         out_specs=(rows, rows, split), check_vma=False)
```

```python
import functools
import jax
import jax.numpy as jnp
from jax import lax
from jax.experimental import pallas as pl
from jax.experimental.pallas import tpu as pltpu
from jax.sharding import PartitionSpec as P

MESH = pl.DeviceIdType.MESH
BF = jnp.bfloat16
F32 = jnp.float32
HEADS, HQ, DV = 8, 128, 192
COLS = 2944
SHARD = 48


def spot():
    dp, sq = lax.axis_index("dp"), lax.axis_index("seq")
    x, zl, c = lax.div(dp, 8), lax.div(lax.rem(dp, 8), 2), lax.rem(dp, 2)
    zh, y = lax.div(sq, 4), lax.rem(sq, 4)
    return x, y, zh * 4 + zl, c


def dev(dx=0, dy=0, dz=0, dc=0):
    x, y, z, c = spot()
    x, y = lax.rem(x + dx + 4, 4), lax.rem(y + dy + 4, 4)
    z, c = lax.rem(z + dz + 16, 16), lax.rem(c + dc, 2)
    return (x * 8 + lax.rem(z, 4) * 2 + c, lax.div(z, 4) * 4 + y)


AXES = {
    "x": ((1, 0, 0), (-1, 0, 0)),
    "y": ((0, 1, 0), (0, -1, 0)),
    "z": ((0, 0, 1), (0, 0, -1)),
}


class Gather:
    def __init__(self, buf, row_of, rows, col, cols, halves, order, send, recv, base, twin=None, direct=False):
        self.buf, self.row_of, self.rows, self.col, self.cols = buf, row_of, rows, col, cols
        self.halves, self.order, self.send, self.recv, self.base = halves, order, send, recv, base
        self.twin, self.direct = twin, direct

    def block(self, ka, kb, part=None):
        r0, nr, c0, nc = part if part else (0, self.rows, 0, self.cols)
        return self.buf.at[pl.ds(pl.multiple_of(self.row_of(ka, kb) + r0, 16), nr), pl.ds(self.col + c0, nc)]

    def copy(self, ka, kb, part, to, slot):
        ref = self.block(ka, kb, part)
        return pltpu.make_async_remote_copy(
            src_ref=ref, dst_ref=ref, send_sem=self.send, recv_sem=self.recv.at[self.base + slot],
            device_id=to, device_id_type=MESH)

    def put(self, ka, kb, part, axis, way, slot):
        if part is not None and (part[1] == 0 or part[3] == 0):
            return
        self.copy(ka, kb, part, dev(*AXES[self.order[axis]][way]), slot).start()

    def far(self, k, axis, slot):
        if self.direct:
            self.copy(k, 0, None, dev(*[2 * d for d in AXES[self.order[axis]][0]]), slot).start()

    def got(self, ka, kb, part, slot):
        if part is not None and (part[1] == 0 or part[3] == 0):
            return
        self.copy(ka, kb, part, dev(*AXES[self.order[0]][0]), slot).wait_recv()

    def share(self, ka, kb):
        if self.twin is None:
            return
        ref = self.block(ka, kb)
        pltpu.make_async_remote_copy(
            src_ref=ref, dst_ref=ref, send_sem=self.twin[0], recv_sem=self.twin[1],
            device_id=dev(0, 0, 0, 1), device_id_type=MESH).start()

    def first(self):
        self.put(0, 0, None, 0, 0, 0)
        self.put(0, 0, None, 0, 1, 1)
        self.far(0, 0, 2)
        self.second(0)
        self.share(0, 0)

    def second(self, k):
        self.put(k, 0, None, 1, 0, 4 + 4 * k)
        self.put(k, 0, None, 1, 1, 5 + 4 * k)
        self.far(k, 1, 6 + 4 * k)

    def a_near(self, k, way):
        self.got(k, 0, None, 0 if k == 3 else 1)
        if not self.direct:
            self.put(k, 0, self.halves[way], 0, way, 2 + way)
        self.second(k)
        self.share(k, 0)

    def a_far(self):
        if self.direct:
            self.got(2, 0, None, 2)
        else:
            self.got(2, 0, self.halves[0], 2)
            self.got(2, 0, self.halves[1], 3)
        self.second(2)
        self.share(2, 0)

    def b_near(self, k, kb, way):
        self.got(k, kb, None, 4 + 4 * k + (0 if kb == 3 else 1))
        if not self.direct:
            self.put(k, kb, self.halves[way], 1, way, 6 + 4 * k + way)
        self.share(k, kb)

    def b_far(self, k):
        if self.direct:
            self.got(k, 2, None, 6 + 4 * k)
        else:
            self.got(k, 2, self.halves[0], 6 + 4 * k)
            self.got(k, 2, self.halves[1], 7 + 4 * k)
        self.share(k, 2)

    def steps(self):
        near = lambda k: [lambda: self.b_near(k, 3, 0), lambda: self.b_near(k, 1, 1)]
        return ([self.first, lambda: self.a_near(3, 0), lambda: self.a_near(1, 1)] + near(0) + [self.a_far]
                + near(3) + near(1) + [lambda: self.b_far(0)] + near(2)
                + [lambda: self.b_far(3), lambda: self.b_far(1), lambda: self.b_far(2)])

    def settle(self):
        ref = self.buf.at[pl.ds(0, 16 * self.rows), pl.ds(self.col, self.cols)]
        pltpu.make_async_copy(ref, ref, self.twin[1]).wait()

    def drain(self):
        ref = self.buf.at[pl.ds(0, 15 * self.rows), pl.ds(self.col, self.cols)]
        pltpu.make_async_copy(ref, ref, self.send).wait()
        if self.twin is not None:
            ref = self.buf.at[pl.ds(0, 16 * self.rows), pl.ds(self.col, self.cols)]
            pltpu.make_async_copy(ref, ref, self.twin[0]).wait()


def col_halves(cols, rows, flip):
    lo = cols // 256 * 128
    if flip:
        lo = cols - lo
    return ((0, rows, 0, lo), (0, rows, lo, cols - lo))


PIECES = ((0, 128, "xz"), (128, 256, "zx"), (384, 512, "zx"), (896, 512, "zx"), (1408, 512, "xz"), (1920, 1024, "zx"))
PLANE = [(dx, 0, dz) for dx in (0, 1, -1, 2) for dz in (0, 1, -1, 2)][1:]
PEERS = [(2, 0, -2), (1, 0, -2), (-1, 0, -2), (0, 0, -2)] + PLANE + [
    (0, 1, 0), (0, -1, 0), (0, 2, 0), (0, 0, 4), (0, 0, -4), (0, 0, 0, 1)]


def nt(a, b):
    return lax.dot_general(a, b, (((1,), (1,)), ((), ())), preferred_element_type=F32)


def tn(a, b):
    return lax.dot_general(a, b, (((0,), (0,)), ((), ())), preferred_element_type=F32)


def hello():
    barrier = pltpu.get_barrier_semaphore()
    for p in PEERS:
        pl.semaphore_signal(barrier, inc=1, device_id=dev(*p), device_id_type=MESH)
    return barrier


def remote(src, dst, send, recv, to):
    return pltpu.make_async_remote_copy(src_ref=src, dst_ref=dst, send_sem=send, recv_sem=recv, device_id=to,
                                        device_id_type=MESH)


def pack(v):
    return jnp.concatenate([v[..., :64, :], v[..., 64:, :]], axis=-1)


def unpack(w):
    return jnp.concatenate([w[..., :64], w[..., 64:]], axis=-2)


class Window:
    def __init__(self, buf, sends, recvs):
        self.buf, self.sends, self.recvs = buf, sends, recvs

    def at(self, kz, half=None):
        x, y, z, c = spot()
        b = self.buf.at[lax.rem(lax.div(z, 4) + kz, 4) * 4 + y]
        return b if half is None else b.at[pl.ds(160 * half, 160)]

    def hop(self, kz, half, up, slot):
        ref = self.at(kz, half)
        return remote(ref, ref, self.sends.at[slot], self.recvs.at[slot], dev(0, 0, 4 if up else -4))

    def across(self, kz, half, dy):
        ref, slot = self.at(kz, half), 6 + (kz * 2 + half) * 3 + dy - 1
        return remote(ref, ref, self.sends.at[slot], self.recvs.at[slot], dev(0, dy))

    def row(self, kz, half):
        for dy in (1, 3, 2):
            self.across(kz, half, dy).start()

    def got(self, kz, half, slot):
        self.hop(kz, half, True, slot).wait_recv()

    def steps(self):
        def s0():
            self.hop(0, 0, True, 0).start()
            self.hop(0, 1, False, 1).start()
            self.hop(0, 1, True, 2).start()
            self.hop(0, 0, False, 3).start()
            self.row(0, 0)
            self.row(0, 1)

        def s1():
            self.got(3, 0, 0)
            self.hop(3, 0, True, 4).start()
            self.row(3, 0)

        def s2():
            self.got(1, 1, 1)
            self.hop(1, 1, False, 5).start()
            self.row(1, 1)

        def s3():
            self.got(3, 1, 2)
            self.row(3, 1)

        def s4():
            self.got(1, 0, 3)
            self.row(1, 0)

        def s5():
            self.got(2, 0, 4)
            self.row(2, 0)
            self.got(2, 1, 5)
            self.row(2, 1)

        return [s0, s1, s2, s3, s4, s5]

    def settle(self, kz):
        for half in (0, 1):
            for dy in (1, 3, 2):
                self.across(kz, half, dy).wait_recv()

    def drain(self):
        for slot in range(30):
            ref = self.at(0, 0)
            remote(ref, ref, self.sends.at[slot], self.recvs.at[slot], dev(0, 1)).wait_send()


def gather_phase(inputs, act, cot, wvs, isem, gain, wall, kvp, normed, rs, q, sends, recvs, twins, ksend, krecv, far, softmax):
    barrier = hello()
    x, y, z, c = spot()
    mine = pl.ds(pl.multiple_of(((x * 4 + lax.rem(z, 4)) * 2 + c) * SHARD, 16), SHARD)
    targets = (act, wall.at[mine, 384:1408], wall.at[mine, 0:128], wvs, wall.at[mine, 1408:2944], cot)
    loads = [pltpu.make_async_copy(a, b, isem.at[i]) for i, (a, b) in enumerate(zip(inputs, targets))]
    for i in (0, 2, 3, 1, 4, 5):
        loads[i].start()
    loads[3].wait()
    wall[mine, 256:384] = jnp.zeros((SHARD, 128), BF)
    wall[mine, 128:320] = wvs[...]
    loads[0].wait()
    wide = act[...].astype(F32)
    r = lax.rsqrt(jnp.mean(wide * wide, axis=-1, keepdims=True) + 1e-6)
    rs[...] = r
    normed[...] = (wide * r * gain[...][None, :]).astype(BF)
    for i in (2, 1, 4, 5):
        loads[i].wait()
    pl.semaphore_wait(barrier, len(PEERS))
    pl.semaphore_signal(far, inc=1, device_id=dev(0, 0, -4), device_id_type=MESH)

    def row(order):
        def of(ka, kb):
            kx, kz = (ka, kb) if order == "xz" else (kb, ka)
            return ((lax.rem(x + kx, 4) * 4 + lax.rem(z + kz, 4)) * 2 + c) * SHARD
        return of

    parts = [Gather(wall, row(o), SHARD, c0, nc, col_halves(nc, SHARD, i % 2), o, sends.at[i], recvs, 20 * i,
                    (twins.at[0, i], twins.at[1, i]), i < 2) for i, (c0, nc, o) in enumerate(PIECES)]
    kvs = [p.steps() for p in parts[:2]]
    bulk = [p.steps() for p in parts[2:]]

    def do(group, i):
        for steps in group:
            steps[i]()

    do(kvs, 0)
    for i in (1, 2, 5):
        do(kvs, i)
    do(bulk, 0)
    for i in (3, 4, 6, 7, 8, 9, 10, 11, 12, 13, 14, 15):
        do(kvs, i)
    parts[0].settle(); parts[1].settle()
    both = jnp.dot(normed[...], wall[:, 0:320], preferred_element_type=F32).astype(BF)
    own = lax.div(z, 4) * 4 + y
    kvp[own, 0:128, :] = both[:, 0:128]
    kvp[own, 128:256, :] = both[:, 128:256]
    kvp[own, 256:320, :] = pack(both[:, 256:320])
    win = Window(kvp, ksend, krecv)
    ks = win.steps()
    ks[0]()
    first, later = bulk[:2], bulk[2:]
    do(first, 1); do(first, 2)
    do(later, 1); do(later, 2)
    ks[1](); ks[2]()
    for i in (3, 4, 5, 6, 7, 8, 9):
        do(first, i)
    ks[3](); ks[4]()
    for i in (3, 4, 5):
        do(later, i)
    ks[5]()
    for i in (10, 11, 12):
        do(first, i)
    for i in (6, 7, 8, 9):
        do(later, i)
    for i in (13, 14, 15):
        do(first, i)
    parts[2].settle(); parts[3].settle()
    qs = (jnp.dot(normed[...], wall[:, 384:1408], preferred_element_type=F32) * HQ ** -0.5).astype(BF)
    for h in range(HEADS):
        q[pl.ds(h * 128, 128), :] = qs[:, h * HQ:(h + 1) * HQ]
    win.settle(0)
    softmax(0)
    for i in (10, 11, 12):
        do(later, i)
    for kz in (3, 1, 2):
        win.settle(kz)
        softmax(kz)
    for i in (13, 14, 15):
        do(later, i)

    for p in parts[4:]:
        p.settle()

    def finish():
        for p in parts:
            p.drain()
        win.drain()
    return finish


def keys_of(kvp, first, n):
    return kvp[pl.ds(first, n), 0:128, :].reshape(n * 128, 128)


def softmax_group(kz, first, q, kvp, v, e, att_of, top, mass):
    rows = pl.ds(pl.multiple_of(first * 128, 512), 512)
    v[rows, 0:128] = kvp[pl.ds(first, 4), 128:256, :].reshape(512, 128)
    v[rows, 128:192] = unpack(kvp[pl.ds(first, 4), 256:320, :]).reshape(512, 64)
    s = nt(keys_of(kvp, first, 4), q[...])
    m = jnp.max(s, axis=0, keepdims=True)
    p = jnp.exp(s - m)
    top[kz:kz + 1, :] = m
    mass[kz:kz + 1, :] = jnp.sum(p, axis=0, keepdims=True)
    pb = p.astype(BF)
    e[rows, :] = pb
    att_of[kz] = jnp.dot(v[rows, :].T, pb, preferred_element_type=F32)


def softmax_join(att_of, top, mass, att, inv):
    part = jnp.exp(top[...] - jnp.max(top[...], axis=0, keepdims=True))
    scale = part / jnp.sum(part * mass[...], axis=0, keepdims=True)
    inv[...] = scale
    att[...] = sum(att_of[k] * scale[k:k + 1, :] for k in range(4))


def value_terms(first, g, e, inv, part):
    rows = pl.ds(pl.multiple_of(first * 128, 512), 512)
    p = (e[rows, :].astype(F32) * inv).astype(BF)
    dv = jnp.dot(p, g[...], preferred_element_type=F32).astype(BF).reshape(4, 128, 192)
    part[pl.ds(first, 4), 0:128, :] = dv[:, :, 0:128]
    part[pl.ds(first, 4), 128:192, :] = pack(dv[:, :, 128:192])


def key_terms(first, q, g, kvp, v, e, inv, centre, part, dqt, start):
    rows = pl.ds(pl.multiple_of(first * 128, 512), 512)
    dp = nt(v[rows, :], g[...])
    ds = (e[rows, :].astype(F32) * inv * (dp - centre[...])).astype(BF)
    part[pl.ds(first, 4)] = jnp.dot(ds, q[...], preferred_element_type=F32).astype(BF).reshape(4, 128, 128)
    term = tn(keys_of(kvp, first, 4), ds)
    if start:
        dqt[...] = term
    else:
        dqt[...] += term


def post(src, dst, sems, to):
    cp = remote(src, dst, sems.at[0], sems.at[1], to)
    cp.start()
    return cp


class Total:
    def __init__(self, part, yfar, ymid, ynear, zs, mid, fbuf, zbuf, wg, cbuf, xs, xbuf, ps, pbuf, hs, hbuf, sems):
        self.part, self.yfar, self.ymid, self.ynear = part, yfar, ymid, ynear
        self.zs, self.mid, self.fbuf, self.zbuf = zs, mid, fbuf, zbuf
        self.wg, self.cbuf, self.xs, self.xbuf, self.ps, self.pbuf = wg, cbuf, xs, xbuf, ps, pbuf
        self.hs, self.hbuf, self.sems = hs, hbuf, sems
        self.rows = part.shape[1]
        self.x, self.y, self.z, self.c = spot()
        self.zh, self.zl = lax.div(self.z, 4), lax.rem(self.z, 4)
        self.yf, self.yc, self.zc = {}, {}, []

    def group(self, k):
        return lax.rem(self.zh + k, 4) * 4

    def block(self, k, d):
        return self.part.at[self.group(k) + lax.rem(self.y + d, 4)]

    def y_out(self, k):
        half = self.rows // 2
        low, high = pl.ds(0, half), pl.ds(half, half)
        sem = [self.sems.at[40 + 6 * k + i] for i in range(6)]
        self.yf[k] = [post(self.block(k, 2).at[low], self.yfar.at[k, 0], sem[0], dev(0, 1)),
                      post(self.block(k, 2).at[high], self.yfar.at[k, 1], sem[1], dev(0, -1))]
        self.yc[k] = [post(self.block(k, 1).at[high], self.ynear.at[k, 0, high], sem[2], dev(0, 1)),
                      post(self.block(k, 3).at[low], self.ynear.at[k, 1, low], sem[3], dev(0, -1))]

    def y_mid(self, k):
        half = self.rows // 2
        for way in (0, 1):
            rows = pl.ds(half * way, half)
            self.yf[k][way].wait()
            own = self.part[self.group(k) + lax.rem(self.y + (3 if way else 1), 4), rows].astype(F32)
            self.ymid[k, way] = (own + self.yfar[k, way].astype(F32)).astype(BF)
            self.yc[k].append(post(self.ymid.at[k, way], self.ynear.at[k, way, rows], self.sems.at[44 + 6 * k + way],
                                   dev(0, -1 if way else 1)))

    def y_in(self, k):
        for cp in self.yc[k]:
            cp.wait()
        f = lambda t: t.astype(F32)
        self.zs[k] = (f(self.part[self.group(k) + self.y]) + f(self.ynear[k, 0]) + f(self.ynear[k, 1])).astype(BF)
        half = self.rows // 2
        low, high = pl.ds(0, half), pl.ds(half, half)
        if k == 2:
            self.fc = [post(self.zs.at[2, low], self.fbuf.at[0], self.sems.at[12], dev(0, 0, 4)),
                       post(self.zs.at[2, high], self.fbuf.at[1], self.sems.at[13], dev(0, 0, -4))]
        if k == 1:
            self.zc.append(post(self.zs.at[1, high], self.zbuf.at[0, high], self.sems.at[14], dev(0, 0, 4)))
        if k == 3:
            self.zc.append(post(self.zs.at[3, low], self.zbuf.at[1, low], self.sems.at[15], dev(0, 0, -4)))

    def z_mid(self, way):
        half = self.rows // 2
        rows = pl.ds(half * way, half)
        self.fc[way].wait()
        self.mid[way] = (self.zs[3 if way else 1, rows].astype(F32) + self.fbuf[way].astype(F32)).astype(BF)
        self.zc.append(post(self.mid.at[way], self.zbuf.at[way, rows], self.sems.at[16 + way], dev(0, 0, -4 if way else 4)))

    def z_in(self):
        for cp in self.zc:
            cp.wait()
        return (self.zs[0].astype(F32) + self.zbuf[0].astype(F32) + self.zbuf[1].astype(F32)).astype(BF)

    def t0(self, normed, grad):
        self.wg[...] = tn(normed[...], grad).astype(BF).reshape(self.wg.shape)
        self.cps = [post(self.wg.at[:, :, 1 - self.c], self.cbuf, self.sems.at[18], dev(0, 0, 0, 1))]

    def wait(self):
        for cp in self.cps:
            cp.wait()

    def t1(self):
        self.wait()
        self.xs[...] = (self.wg[:, :, self.c].astype(F32) + self.cbuf[...].astype(F32)).astype(BF)
        self.cps = [post(self.xs.at[lax.rem(self.x + dx + 4, 4), lax.rem(self.zl + dz + 4, 4)], self.xbuf.at[i],
                         self.sems.at[19 + i], dev(dx, 0, dz)) for i, (dx, _, dz) in enumerate(PLANE)]

    def t2(self):
        self.wait()
        total = self.xs[self.x, self.zl].astype(F32)
        for i in range(15):
            total += self.xbuf[i].astype(F32)
        self.ps[...] = total.astype(BF)
        self.cps = [post(self.ps, self.pbuf.at[k - 1], self.sems.at[33 + k], dev(0, 0, 4 * k)) for k in (2, 1, 3)]

    def t3(self):
        self.wait()
        self.hs[...] = in_order(self.ps, self.pbuf, self.zh).astype(BF)
        self.cps = [post(self.hs, self.hbuf.at[d - 1], self.sems.at[36 + d], dev(0, d)) for d in (1, 3, 2)]

    def t4(self):
        self.wait()
        return in_order(self.hs, self.hbuf, self.y)


def in_order(mine, others, place):
    total = None
    for i in range(4):
        d = lax.rem(place - i + 4, 4)
        term = mine[...].astype(F32)
        for j in (1, 2, 3):
            term = jnp.where(d == j, others[j - 1].astype(F32), term)
        total = term if total is None else total + term
    return total


def body(act_in, gain, wq, wk, wv, wo, cot_in, out, ingrad, wgrad,
         act, cot, wvs, isem, wall, kvp, normed, rs, q, g, v, e, att_of, top, mass, att, inv, centre, dqt, rows_of, ng,
         sends, recvs, twins, ksend, krecv, far, *slabs):
    half = len(slabs) // 2
    K, V = Total(*slabs[:half]), Total(*slabs[half:])
    finish = gather_phase((act_in, wq, wk, wv, wo, cot_in), act, cot, wvs, isem, gain, wall, kvp, normed, rs, q, sends, recvs, twins,
                 ksend, krecv, far, lambda kz: softmax_group(kz, K.group(kz), q, kvp, v, e, att_of, top, mass))
    for h in range(HEADS):
        g[pl.ds(h * 128, 128), :] = nt(cot[...], wall[pl.ds(h * DV, DV), 1408:2944]).astype(BF)
    softmax_join(att_of, top, mass, att, inv)

    for k in (2, 1, 3, 0):
        value_terms(V.group(k), g, e, inv[k:k + 1, :], V.part)
        V.y_out(k)
    centre[...] = jnp.sum(att[...] * g[...].astype(F32).T, axis=0, keepdims=True)

    def keys(k):
        key_terms(K.group(k), q, g, kvp, v, e, inv[k:k + 1, :], centre, K.part, dqt, k == 2)
        K.y_out(k)

    keys(2)
    V.y_mid(2)
    V.y_mid(1)
    keys(1)
    V.y_mid(3)
    V.y_mid(0)
    V.y_in(2)
    keys(3)
    V.y_in(1)
    V.y_in(3)
    K.y_mid(2)
    keys(0)
    K.y_mid(1)
    for h in range(HEADS):
        rows_of[:, h * HQ:(h + 1) * HQ] = (dqt[:, h * 128:(h + 1) * 128].T * HQ ** -0.5).astype(BF)
    K.y_in(2)
    K.y_mid(3)
    K.y_mid(0)
    V.z_mid(0)
    V.z_mid(1)
    ng[...] = nt(rows_of[:, 0:1024], wall[:, 384:1408])
    V.y_in(0)
    K.y_in(1)
    K.y_in(3)
    K.z_mid(0)
    K.z_mid(1)
    K.y_in(0)
    for h in range(0, HEADS, 2):
        pair = att[:, h * 128:(h + 2) * 128].T.astype(BF)
        rows_of[:, h * DV:(h + 2) * DV] = jnp.concatenate([pair[:128], pair[128:]], axis=1)
    a, r = act[...].astype(F32), rs[...]
    out[...] = (a + jnp.dot(rows_of[...], wall[:, 1408:2944], preferred_element_type=F32)).astype(BF)
    vsum = V.z_in()
    vgrad = jnp.concatenate([vsum[0:128], unpack(vsum[128:192])], axis=1)
    V.t0(normed, jnp.concatenate([vgrad, jnp.zeros((128, 64), BF)], axis=1))
    V.t1()
    kgrad = K.z_in()
    K.t0(normed, kgrad)
    scaled = (ng[...] + nt(jnp.concatenate([kgrad, vgrad], axis=1), wall[:, 0:320])) * gain[...][None, :]
    K.t1()
    inner = jnp.mean(scaled * a, axis=-1, keepdims=True)
    ingrad[...] = (cot[...].astype(F32) + r * (scaled - a * r * r * inner)).astype(BF)
    pl.semaphore_wait(far, 1)
    V.t2()
    K.t2()
    V.t3()
    K.t3()
    finish()
    wgrad[:, 128:320] = V.t4()[:, 0:192]
    wgrad[:, 0:128] = K.t4()


def hand_over(a, b, c, to_a, to_b, to_c):
    to_a[...] = a[...]
    to_b[...] = b[...]
    to_c[...] = c[...]


def per_device(act, gain, wq, wk, wv, wo, cot):
    vm, hbm = pl.BlockSpec(memory_space=pltpu.VMEM), pl.BlockSpec(memory_space=pl.ANY)
    V, DMA = pltpu.VMEM, pltpu.SemaphoreType.DMA
    def slab(rows, cols):
        return [V((16, rows, 128), BF), V((4, 2, rows // 2, 128), BF), V((4, 2, rows // 2, 128), BF),
                V((4, 2, rows, 128), BF), V((4, rows, 128), BF), V((2, rows // 2, 128), BF),
                V((2, rows // 2, 128), BF), V((2, rows, 128), BF), V((4, 4, 2, SHARD, cols), BF), V((4, 4, SHARD, cols), BF),
                V((4, 4, SHARD, cols), BF), V((15, SHARD, cols), BF), V((SHARD, cols), BF), V((3, SHARD, cols), BF),
                V((SHARD, cols), BF), V((3, SHARD, cols), BF), DMA((64, 2))]

    scratch = [
        V((128, 1536), BF), V((128, 1536), BF), V((SHARD, DV), BF), DMA((6,)),
        V((1536, COLS), BF), V((16, 320, 128), BF), V((128, 1536), BF), V((128, 1), F32), V((1024, 128), BF), V((1024, 192), BF),
        V((2048, 192), BF), V((2048, 1024), BF), V((4, 192, 1024), F32), V((4, 1024), F32), V((4, 1024), F32),
        V((192, 1024), F32), V((4, 1024), F32), V((1, 1024), F32),
        V((128, 1024), F32), V((128, 1536), BF), V((128, 1536), F32),
        DMA((6,)), DMA((120,)), DMA((2, 6)), DMA((30,)), DMA((30,)), pltpu.SemaphoreType.REGULAR,
    ] + slab(128, 128) + slab(192, 256)
    o, i, w = pl.pallas_call(
        body,
        out_shape=(jax.ShapeDtypeStruct((128, 1536), BF), jax.ShapeDtypeStruct((128, 1536), BF),
                   jax.ShapeDtypeStruct((SHARD, 320), F32)),
        in_specs=[hbm, vm, hbm, hbm, hbm, hbm, hbm], out_specs=(vm,) * 3, scratch_shapes=scratch,
        compiler_params=pltpu.CompilerParams(collective_id=0, has_side_effects=True, vmem_limit_bytes=58 * 2**20),
        name="layer",
    )(act[0], gain, wq, wk, wv, wo, cot[0])
    o, i, w = pl.pallas_call(
        hand_over,
        out_shape=(jax.ShapeDtypeStruct((128, 1536), BF), jax.ShapeDtypeStruct((128, 1536), BF),
                   jax.ShapeDtypeStruct((SHARD, 320), F32)),
        in_specs=[vm] * 3, out_specs=(vm,) * 3, name="hand_over",
    )(o, i, w)
    return o[None], i[None], w


def solution(mesh):
    rows = P("dp", "seq", None)
    split = P("dp", None)
    return jax.shard_map(per_device, mesh=mesh, in_specs=(rows, P(), split, split, split, split, rows),
                         out_specs=(rows, rows, split), check_vma=False)
```
